256 devices in a mesh: seq: 64 (over z_lo, x, y, core), dp: 4 (over z_hi).
Axes of the slice: x: 4, y: 4, z: 8 (z_hi: 4, z_lo: 2; z = z_hi * 2 + z_lo), core: 2. Of those that a mesh axis runs over, the one named last changes fastest.
Arguments:
- tokens: bfloat16 [4, 262144, 256], P('dp', 'seq'), may hold values from -6 to 6
- cotangent: bfloat16 [4, 262144, 256], P('dp', 'seq'), may hold values from -6 to 6
- first_factor: bfloat16 [512, 512, 512], P('seq', 'dp'), may hold values from -0.25 to 0.25
- second_factor: bfloat16 [512, 512, 512], P('seq', 'dp'), may hold values from -0.25 to 0.25
- hidden_weight: bfloat16 [256, 768], replicated, may hold values from -0.375 to 0.375
- output_weight: bfloat16 [768, 256], replicated, may hold values from -0.21875 to 0.21875
Outputs:
- output: bfloat16 [4, 262144, 256], P('dp', 'seq')
- first_grad: bfloat16 [512, 512, 512], P('seq', 'dp')
- second_grad: bfloat16 [512, 512, 512], P('seq', 'dp')
- hidden_grad: float32 [256, 768], replicated
- output_grad: float32 [768, 256], replicated
The draws below stay inside these ranges and needn't reach their ends.
All inputs are finite; a program needn't handle non-finite values.
Results may differ from the reference program's by a relative error of at most 0.017.
Values may be sent and summed in bfloat16 or wider, within the bound.
A program may use at most 128 MiB of HBM per device.

```python
import math
import jax
import jax.numpy as jnp
from jax import lax

BLK = 512
C = 256
FF = 768
LENGTH = 262144
DOCS = 4


def steps_of(rng, dims, pieces, least, top_value):
    def one(dim, shards_of):
        draws = jax.random.uniform(jax.random.fold_in(jax.random.fold_in(rng, 6), dim), (shards_of,), jnp.float32, least / len(pieces), top_value / len(pieces))
        return jnp.repeat(jnp.exp(draws), dims[dim] // shards_of).reshape((-1,) + (1,) * (len(dims) - dim - 1))

    loudness = one(*pieces[0])
    for cut in pieces[1:]:
        loudness = loudness * one(*cut)
    return loudness


def centred(rng, extent, spread, most, pieces=(), kind=jnp.bfloat16):
    loudness = steps_of(rng, extent, pieces, -0.22, 0.18) if pieces else 1.0
    array = jax.random.normal(rng, extent, jnp.float32) * spread * loudness
    return jnp.minimum(jnp.maximum(array, -most), most).astype(kind)


def setup_inputs(seed: int = 0) -> dict:
    splits = jax.random.split(jax.random.key(seed), 7)
    tokens = centred(splits[0], (DOCS, LENGTH, C), 1.0, 6.0, ((0, 4), (1, 64)))
    cotangent = centred(splits[1], (DOCS, LENGTH, C), 1.0, 6.0, ((0, 4), (1, 64)))
    first_factor = centred(splits[2], (BLK, BLK, BLK), BLK ** -0.5, 0.25, ((0, 64), (1, 4)))
    second_factor = centred(splits[3], (BLK, BLK, BLK), BLK ** -0.5, 0.25, ((0, 64), (1, 4)))
    hidden_weight = centred(splits[4], (C, FF), C ** -0.5, 0.375)
    output_weight = centred(splits[5], (FF, C), FF ** -0.5, 0.21875)
    return {"tokens": tokens, "cotangent": cotangent, "first_factor": first_factor, "second_factor": second_factor, "hidden_weight": hidden_weight, "output_weight": output_weight}


def gelu_tanh(value):
    return jax.nn.gelu(value, approximate=True)

def token_work(mixed, inputs, grads, hidden_weight, output_weight):
    gate = jax.nn.silu(inputs.astype(jnp.float32))
    gated = (mixed.astype(jnp.float32) * gate).astype(jnp.bfloat16)
    pre = jnp.dot(gated, hidden_weight, preferred_element_type=jnp.float32)
    active_f, gelu_back = jax.vjp(gelu_tanh, pre)
    activated = active_f.astype(jnp.bfloat16)
    output = (gated.astype(jnp.float32) + jnp.dot(activated, output_weight, preferred_element_type=jnp.float32)).astype(jnp.bfloat16)
    back = jnp.dot(grads, output_weight.T, preferred_element_type=jnp.float32)
    d_hidden = gelu_back(back)[0].astype(jnp.bfloat16)
    out_part = jnp.dot(activated.T, grads, preferred_element_type=jnp.float32)
    hid_part = jnp.dot(gated.T, d_hidden, preferred_element_type=jnp.float32)
    d_gated = grads.astype(jnp.float32) + jnp.dot(d_hidden, hidden_weight.T, preferred_element_type=jnp.float32)
    d_mixed = (d_gated * gate).astype(jnp.bfloat16)
    return (output, d_mixed, hid_part, out_part)

def rounded(value):
    return lax.optimization_barrier(value.astype(jnp.bfloat16)).astype(jnp.float32)

def reference(tokens, cotangent, first_factor, second_factor, hidden_weight, output_weight):
    first_wide = first_factor.astype(jnp.float32)
    second_wide = second_factor.astype(jnp.float32)

    def per_document(carry, pair):
        inputs, grads = pair
        sum_first, sum_second, sum_hidden, sum_output = carry
        blocks = inputs.reshape(BLK, BLK, C).astype(jnp.float32)
        first_mixed = jnp.einsum('akb,abc->akc', first_wide, blocks).astype(jnp.bfloat16)
        first_cols = first_mixed.astype(jnp.float32)
        mixed = jnp.einsum('kla,akc->lkc', second_wide, first_cols).astype(jnp.bfloat16).reshape(LENGTH, C)
        output, d_mixed, hid_part, out_part = token_work(mixed, inputs, grads, hidden_weight, output_weight)
        d_cols = d_mixed.reshape(BLK, BLK, C).astype(jnp.float32)
        part_second = rounded(jnp.einsum('lkc,akc->kla', d_cols, first_cols))
        d_first = jnp.einsum('kla,lkc->akc', second_wide, d_cols).astype(jnp.bfloat16)
        part_first = rounded(jnp.einsum('akc,abc->akb', d_first.astype(jnp.float32), blocks))
        carry = (sum_first + part_first, sum_second + part_second, sum_hidden + hid_part, sum_output + out_part)
        return (carry, output)
    start = (jnp.zeros((BLK, BLK, BLK), jnp.float32), jnp.zeros((BLK, BLK, BLK), jnp.float32), jnp.zeros((C, FF), jnp.float32), jnp.zeros((FF, C), jnp.float32))
    carry, outputs = lax.scan(per_document, start, (tokens, cotangent))
    block_scale = 1.0 / math.sqrt(DOCS * C)
    weight_scale = 1.0 / math.sqrt(DOCS * LENGTH)
    first_grad = (carry[0] * block_scale).astype(jnp.bfloat16)
    second_grad = (carry[1] * block_scale).astype(jnp.bfloat16)
    return (outputs, first_grad, second_grad, carry[2] * weight_scale, carry[3] * weight_scale)
```

```python
import functools
import math

import jax
import jax.numpy as jnp
from jax import lax
from jax.experimental import pallas as pl
from jax.experimental.pallas import tpu as pltpu
from jax.sharding import PartitionSpec as P

MESH = pl.DeviceIdType.MESH
BF = jnp.bfloat16
F32 = jnp.float32
DMA = pltpu.SemaphoreType.DMA
ANY = pl.BlockSpec(memory_space=pl.ANY)
VM = pl.BlockSpec(memory_space=pltpu.VMEM)
BLOCK_SCALE = 1.0 / math.sqrt(1024.0)
WEIGHT_SCALE = 1.0 / math.sqrt(1048576.0)


def dev(s, p):
    return {"seq": s, "dp": p}


def offset(s, i):
    z, x, y, c = s // 32, (s // 8) % 4, (s // 2) % 4, s % 2
    j = i // 2
    z = (z + i) % 2
    x = (x + j) % 4
    y = (y + j // 4 + j) % 4
    c = (c + j // 16) % 2
    return z * 32 + x * 8 + y * 2 + c


def place():
    s, p = lax.axis_index("seq"), lax.axis_index("dp")
    z, b = s // 32, (s // 16) % 2
    mate = p + 1 - 2 * (p % 2)
    twin = s + 16 * (1 - 2 * b)
    same = (z + b) % 2 == (p + p // 2) % 2
    return s, p, z, b, mate, 3 - p, twin, same


def remote(src, dst, ssem, rsem, s, p):
    return pltpu.make_async_remote_copy(src, dst, ssem, rsem, device_id=dev(s, p), device_id_type=MESH)


def drain(ref, sem):
    pltpu.make_async_copy(ref, ref, sem).wait()


def loop(n, body, start=0):
    def step(i, carry):
        body(i)
        return carry

    lax.fori_loop(start, n, step, 0)


def dot(a, b, dims=((1,), (0,))):
    return lax.dot_general(a, b, (dims, ((), ())), preferred_element_type=F32)


def front_kernel(
    x_ref, f_ref, s_ref, perm_ref, fm_ref, sp_ref, xp_ref,
    xown, xmate, f2, fmx, out, load, xs, xr, fs, fr, sas, sar, sbs, sbr, ms, mr, tail,
):
    s, p, z, b, mate, cross, twin, same = place()
    side = p // 2
    odd = p % 2
    pltpu.make_async_copy(x_ref, xown, load.at[0]).start()
    pltpu.make_async_copy(f_ref, f2.at[:, side], load.at[1]).start()
    bar = pltpu.get_barrier_semaphore()

    def greet(t, q):
        pl.semaphore_signal(bar, 1, device_id=dev(t, q), device_id_type=MESH)

    greet(s, mate)
    greet(s, cross)
    greet(twin, mate)
    loop(64, lambda i: greet(offset(s, i), p), 1)
    pl.semaphore_wait(bar, 66)

    remote(f_ref, f2.at[:, side], fs, fr, s, cross).start()
    dest = jnp.where(same, p, mate)
    remote(s_ref.at[1 - b], sp_ref.at[:, p], sas.at[0], sar, twin, dest).start()

    @pl.when(same)
    def _():
        pltpu.make_async_copy(s_ref.at[b], sp_ref.at[:, p], sar).start()

    @pl.when(jnp.logical_not(same))
    def _():
        remote(s_ref.at[b], sp_ref.at[:, p], sas.at[1], sar, s, mate).start()

    loop(8, lambda a: remote(x_ref.at[a], xmate.at[a], xs, xr.at[a], s, mate).start())

    def mix(e, x):
        def one(a):
            fmx[a] = dot(f2[a].reshape(256, 512), x[a]).astype(BF)

        return one

    def spread(e):
        def group(g):
            rows = fmx[:, pl.ds(pl.multiple_of(g * 32, 32), 32), :].reshape(256, 256)
            turned = dot(perm_ref[...], rows).astype(BF).reshape(8, 32, 256)
            out[e, pl.ds(g * 8, 8)] = turned

        loop(8, group)
        pltpu.make_async_copy(out.at[e, s], fm_ref.at[e, s], mr).start()

        def send(i):
            t = offset(s, i)
            remote(out.at[e, t], fm_ref.at[e, s], ms, mr, t, p).start()

        loop(64, send, 1)

    pltpu.make_async_copy(x_ref, xown, load.at[0]).wait()
    pltpu.make_async_copy(f_ref, f2.at[:, side], load.at[1]).wait()
    drain(f2.at[:, 1 - side], fr)
    loop(8, mix(odd, xown))
    spread(odd)
    drain(sp_ref.at[:, pl.ds(0, 2)], sar)
    half = sp_ref.at[:, pl.ds(2 * side, 2)]
    remote(half, half, sbs, sbr, s, cross).start()

    def arrive(a):
        drain(xmate.at[a], xr.at[a])
        pltpu.make_async_copy(xmate.at[a], xp_ref.at[a], tail).start()
        mix(1 - odd, xmate)(a)

    loop(8, arrive)
    spread(1 - odd)
    drain(x_ref, xs)
    drain(f_ref, fs)
    drain(s_ref.at[0], sas.at[0])

    @pl.when(jnp.logical_not(same))
    def _():
        drain(s_ref.at[0], sas.at[1])

    drain(xmate, tail)
    drain(sp_ref.at[:, pl.ds(0, 2)], sbs)
    drain(sp_ref.at[:, pl.ds(0, 2)], sbr)
    drain(out.at[:, pl.ds(0, 63)], ms)
    drain(out, mr)


def front(x, f, second, perm):
    return pl.pallas_call(
        front_kernel,
        out_shape=(
            jax.ShapeDtypeStruct((2, 64, 32, 256), BF),
            jax.ShapeDtypeStruct((4, 4, 128, 512), BF),
            jax.ShapeDtypeStruct((8, 512, 256), BF),
        ),
        in_specs=[ANY, ANY, ANY, VM],
        out_specs=(ANY, ANY, ANY),
        scratch_shapes=[
            pltpu.VMEM((8, 512, 256), BF),
            pltpu.VMEM((8, 512, 256), BF),
            pltpu.VMEM((8, 2, 128, 512), BF),
            pltpu.VMEM((8, 256, 256), BF),
            pltpu.VMEM((2, 64, 32, 256), BF),
            DMA((2,)), DMA, DMA((8,)), DMA, DMA, DMA((2,)), DMA, DMA, DMA, DMA, DMA, DMA,
        ],
        compiler_params=pltpu.CompilerParams(
            collective_id=1, has_side_effects=True, vmem_limit_bytes=40 << 20
        ),
    )(x, f, second, perm)


def token_tile(mixed, x, grads, w1, w2, w1t, w2t):
    xf = x.astype(F32)
    gate = xf / (1.0 + jnp.exp(-xf))
    gated = (mixed.astype(F32) * gate).astype(BF)
    pre = dot(gated, w1)
    root = math.sqrt(2.0 / math.pi)
    square = pre * pre
    tanh = jnp.tanh(pre * (root + (root * 0.044715) * square))
    half = 0.5 * (1.0 + tanh)
    activated = (pre * half).astype(BF)
    slope = half + 0.5 * pre * (1.0 - tanh * tanh) * (root + (3.0 * root * 0.044715) * square)
    output = (gated.astype(F32) + dot(activated, w2)).astype(BF)
    d_hidden = (dot(grads, w2t) * slope).astype(BF)
    out_part = dot(grads, activated, ((0,), (0,)))
    hid_part = dot(gated, d_hidden, ((0,), (0,)))
    d_mixed = ((grads.astype(F32) + dot(d_hidden, w1t)) * gate).astype(BF)
    return output, d_mixed, hid_part, out_part


def back_kernel(
    fm_ref, sp_ref, xo_ref, xp_ref, xt_ref, ct_ref, w1, w2, w1t, w2t, perm_ref,
    out_ref, fg_ref, sg_ref, wg_ref,
    fm, sp, xe, xt, ct, fmk, dmk, mb, mr, db, dr, ob, dfb, dfr, dfa, gb, gr, go, fgb, fgr, fgo,
    acc, rsb, zb, agb,
    load, mbs, mrs, dbs, drs, dfbs, dfrs, gbs, grs, gos, gor, fgs, fgrs, rss, rsr, zbs, zbr, ags, agr, tail,
):
    s, p, z, b, mate, cross, twin, same = place()
    side, odd = p // 2, p % 2
    kind = (p + p // 2) % 2
    base = 2 * side
    copies = [
        (fm_ref, fm), (sp_ref, sp), (xt_ref, xt), (ct_ref, ct),
        (xo_ref, xe.at[:, :, pl.ds(pl.multiple_of(256 * odd, 256), 256)]),
        (xp_ref, xe.at[:, :, pl.ds(pl.multiple_of(256 * (1 - odd), 256), 256)]),
    ]
    for n, (src, dst) in enumerate(copies):
        pltpu.make_async_copy(src, dst, load.at[n]).start()

    def loaded(n):
        pltpu.make_async_copy(copies[n][0], copies[n][1], load.at[n]).wait()

    bar = pltpu.get_barrier_semaphore()

    def greet(t, q):
        pl.semaphore_signal(bar, 1, device_id=dev(t, q), device_id_type=MESH)

    flip = s + 32 * (1 - 2 * z)
    for q in (2 - base, 3 - base):
        greet(s, q)
        greet(flip, q)
    greet(s, mate)

    def hello(i):
        greet(offset(s, i), p)
        greet(offset(s, i), mate)

    loop(64, hello, 1)

    loaded(0)
    loaded(1)

    def columns(src, dst, n):
        def piece(t):
            for e in range(2):
                rows = src(e, t).astype(F32)
                for i in range(2):
                    dst[n + i, pl.ds(pl.multiple_of(t * 128, 128), 128), 256 * e:256 * e + 256] = (
                        rows[:, 8 * i:8 * i + 8, :].reshape(128, 256).astype(BF)
                    )

        loop(4, piece)

    for j in range(2):
        columns(lambda e, t: fm[e, pl.ds(t * 16, 16), 16 * j:16 * j + 16, :], fmk, 2 * j)
    pl.semaphore_wait(bar, 131)

    for j in range(2):
        def second(t):
            parts = [
                dot(sp[2 * j + i, t], fmk[2 * j + i]).reshape(16, 8, 512) for i in range(2)
            ]
            whole = jnp.concatenate(parts, axis=1).astype(BF)
            for e in range(2):
                mb[j, pl.ds(t * 16, 16), e] = whole[:, :, 256 * e:256 * e + 256]

        loop(4, second)
        pltpu.make_async_copy(mb.at[j, s, odd], mr.at[j, kind, s // 8, s % 8], mrs.at[j]).start()

        def send(i):
            t = offset(s, i)
            remote(mb.at[j, t, 1 - odd], mr.at[j, kind, s // 8, s % 8], mbs.at[j], mrs.at[j], t, mate).start()

            @pl.when(i > 0)
            def _():
                remote(mb.at[j, t, odd], mr.at[j, kind, s // 8, s % 8], mbs.at[j], mrs.at[j], t, p).start()

        loop(64, send)

    acc[...] = jnp.zeros_like(acc)
    loaded(2)
    loaded(3)
    for j in range(2):
        drain(mr.at[j], mrs.at[j])

        def tile(n):
            lo = (s + n) % 8
            mixed = mr[j, :, :, lo].reshape(256, 256)
            x = xt[j, :, :, lo].reshape(256, 256)
            grads = ct[j, :, :, lo].reshape(256, 256)
            output, d_mixed, hid_part, out_part = token_tile(
                mixed, x, grads, w1[...], w2[...], w1t[...], w2t[...]
            )
            ob[j, :, :, lo] = output.reshape(2, 8, 16, 256)
            db[j, :, :, lo] = d_mixed.reshape(2, 8, 16, 256)
            acc[0:16] += hid_part.reshape(16, 16, 768)
            acc[16:32] += out_part.reshape(16, 16, 768)

            def send(m):
                hi = (s // 8 + m) % 8
                t = hi * 8 + lo
                remote(db.at[j, 1 - kind, hi, lo], dr.at[j, odd, s], dbs.at[j], drs.at[j], t, mate).start()
                here = t == s

                @pl.when(here)
                def _():
                    pltpu.make_async_copy(db.at[j, kind, hi, lo], dr.at[j, odd, s], drs.at[j]).start()

                @pl.when(jnp.logical_not(here))
                def _():
                    remote(db.at[j, kind, hi, lo], dr.at[j, odd, s], dbs.at[j], drs.at[j], t, p).start()

            loop(8, send)

        loop(8, tile)
        pltpu.make_async_copy(ob.at[j], out_ref.at[j], tail.at[0]).start()

    w = s % 32
    pltpu.make_async_copy(acc.at[w], rsb.at[w], rsr).start()

    def scatter(i):
        t = (w + i) % 32
        remote(acc.at[t], rsb.at[w], rss, rsr, z * 32 + t, p).start()

    loop(32, scatter, 1)

    for j in range(2):
        drain(dr.at[j], drs.at[j])
        columns(lambda e, t: dr[j, e, pl.ds(t * 16, 16)], dmk, 0)

        def grads_of(t):
            for i in range(2):
                rows = dmk[i, pl.ds(pl.multiple_of(t * 128, 128), 128), :]
                gb[2 * j + i, t] = dot(rows, fmk[2 * j + i], ((1,), (1,))).astype(BF)

        loop(4, grads_of)
        remote(
            gb.at[pl.ds(2 * j, 2), pl.ds(2 - base, 2)], gr.at[pl.ds(2 * j, 2)],
            gbs.at[j], grs.at[j], s, cross,
        ).start()

        def first_back(t):
            parts = []
            for i in range(2):
                weights = sp[2 * j + i, :, :, pl.ds(pl.multiple_of(t * 128, 128), 128)].reshape(512, 128)
                parts.append(dot(weights, dmk[i], ((0,), (0,))).reshape(16, 8, 512))
            whole = jnp.concatenate(parts, axis=1).astype(BF)
            for e in range(2):
                dfb[j, pl.ds(t * 16, 16), e] = whole[:, :, 256 * e:256 * e + 256]

        loop(4, first_back)
        pltpu.make_async_copy(dfb.at[j, s], dfr.at[j, s], dfrs.at[j]).start()

        def send(i):
            t = offset(s, i)
            remote(dfb.at[j, t], dfr.at[j, s], dfbs.at[j], dfrs.at[j], t, p).start()

        loop(64, send, 1)

    drain(rsb, rsr)
    plane = 2 * p + z
    zb[plane] = jnp.sum(rsb[...], axis=0)
    for q in range(4):
        for u in range(2):
            @pl.when(plane != 2 * q + u)
            def _():
                remote(zb.at[plane], zb.at[plane], zbs, zbr, u * 32 + w, q).start()

    loaded(4)
    loaded(5)
    for j in range(2):
        drain(dfr.at[j], dfrs.at[j])

        def turn(g):
            for e in range(2):
                rows = dfr[j, pl.ds(g * 16, 16), e].reshape(256, 256)
                turned = dot(perm_ref[...], rows).astype(BF).reshape(8, 32, 256)
                dfa[:, pl.ds(pl.multiple_of(g * 32, 32), 32), 256 * e:256 * e + 256] = turned

        loop(4, turn)

        def first_grad(a):
            fgb[j, a] = dot(dfa[a], xe[a], ((1,), (1,))).astype(BF).reshape(2, 64, 512)

        loop(8, first_grad)
        remote(fgb.at[j, :, 1 - side], fgr.at[j], fgs.at[j], fgrs.at[j], s, cross).start()

    drain(zb.at[pl.ds(0, 7)], zbr)
    agb[w] = jnp.sum(zb[...], axis=0) * WEIGHT_SCALE

    def gather(i):
        remote(agb.at[w], agb.at[w], ags, agr, z * 32 + (w + i) % 32, p).start()

    loop(32, gather, 1)

    for j in range(2):
        drain(gr.at[pl.ds(2 * j, 2)], grs.at[j])

    def second_sum(k):
        mine = gb[k, pl.ds(base, 2)].astype(F32)
        go[k] = ((mine + gr[k].astype(F32)) * BLOCK_SCALE).astype(BF)

    loop(4, second_sum)
    home = jnp.where(same, s, twin)
    remote(go.at[:, 1 - odd], sg_ref.at[b], gos.at[0], gor, home, mate).start()

    @pl.when(same)
    def _():
        pltpu.make_async_copy(go.at[:, odd], sg_ref.at[b], gor).start()

    @pl.when(jnp.logical_not(same))
    def _():
        remote(go.at[:, odd], sg_ref.at[b], gos.at[1], gor, twin, p).start()

    for j in range(2):
        drain(fgr.at[j], fgrs.at[j])

        def first_sum(a):
            mine = fgb[j, a, side].astype(F32)
            fgo[j, a] = ((mine + fgr[j, a].astype(F32)) * BLOCK_SCALE).astype(BF)

        loop(8, first_sum)
    pltpu.make_async_copy(fgo, fg_ref, tail.at[1]).start()
    drain(agb.at[pl.ds(0, 31)], agr)
    pltpu.make_async_copy(agb, wg_ref, tail.at[2]).start()

    for j in range(2):
        drain(mr.at[j, 0], mbs.at[j])
        drain(mr.at[j, 0, pl.ds(0, 7)], mbs.at[j])
        drain(mr.at[j, 0, 0, pl.ds(0, 7)], mbs.at[j])
        drain(mr.at[j, 0], dbs.at[j])
        drain(mr.at[j, 0, pl.ds(0, 7)], dbs.at[j])
        drain(mr.at[j, 0, 0, pl.ds(0, 7)], dbs.at[j])
        drain(dfb.at[j, pl.ds(0, 63)], dfbs.at[j])
        drain(gr.at[pl.ds(2 * j, 2)], gbs.at[j])
        drain(fgr.at[j], fgs.at[j])
    drain(rsb.at[pl.ds(0, 31)], rss)
    drain(zb.at[pl.ds(0, 7)], zbs)
    drain(agb.at[pl.ds(0, 31)], ags)
    drain(go.at[:, 0], gos.at[0])

    @pl.when(jnp.logical_not(same))
    def _():
        drain(go.at[:, 0], gos.at[1])

    drain(sg_ref, gor)
    drain(ob, tail.at[0])
    drain(fgo, tail.at[1])
    drain(agb, tail.at[2])


def back(fm, sp, xo, xp, xt, ct, w1, w2, w1t, w2t, perm):
    half = (2, 2, 8, 8, 16, 256)
    return pl.pallas_call(
        back_kernel,
        out_shape=(
            jax.ShapeDtypeStruct(half, BF),
            jax.ShapeDtypeStruct((2, 8, 64, 512), BF),
            jax.ShapeDtypeStruct((2, 4, 128, 512), BF),
            jax.ShapeDtypeStruct((32, 16, 768), F32),
        ),
        in_specs=[ANY] * 6 + [VM] * 5,
        out_specs=(ANY,) * 4,
        scratch_shapes=[
            pltpu.VMEM((2, 64, 32, 256), BF),
            pltpu.VMEM((4, 4, 128, 512), BF),
            pltpu.VMEM((8, 512, 512), BF),
            pltpu.VMEM(half, BF),
            pltpu.VMEM(half, BF),
            pltpu.VMEM((4, 512, 512), BF),
            pltpu.VMEM((2, 512, 512), BF),
            pltpu.VMEM((2, 64, 2, 16, 256), BF),
            pltpu.VMEM(half, BF),
            pltpu.VMEM(half, BF),
            pltpu.VMEM((2, 2, 64, 16, 256), BF),
            pltpu.VMEM(half, BF),
            pltpu.VMEM((2, 64, 2, 16, 256), BF),
            pltpu.VMEM((2, 64, 2, 16, 256), BF),
            pltpu.VMEM((8, 128, 512), BF),
            pltpu.VMEM((4, 4, 128, 512), BF),
            pltpu.VMEM((4, 2, 128, 512), BF),
            pltpu.VMEM((4, 2, 128, 512), BF),
            pltpu.VMEM((2, 8, 2, 64, 512), BF),
            pltpu.VMEM((2, 8, 64, 512), BF),
            pltpu.VMEM((2, 8, 64, 512), BF),
            pltpu.VMEM((32, 16, 768), F32),
            pltpu.VMEM((32, 16, 768), F32),
            pltpu.VMEM((8, 16, 768), F32),
            pltpu.VMEM((32, 16, 768), F32),
            DMA((6,)), DMA((2,)), DMA((2,)), DMA((2,)), DMA((2,)), DMA((2,)), DMA((2,)),
            DMA((2,)), DMA((2,)), DMA((2,)), DMA, DMA((2,)), DMA((2,)),
            DMA, DMA, DMA, DMA, DMA, DMA, DMA((3,)),
        ],
        compiler_params=pltpu.CompilerParams(
            collective_id=2, has_side_effects=True, vmem_limit_bytes=58 << 20
        ),
    )(fm, sp, xo, xp, xt, ct, w1, w2, w1t, w2t, perm)


def by_column(rows):
    parts = rows.reshape(8, 4, 16, 2, 2, 2, 256)
    parts = jnp.concatenate([parts[:, 0:1], parts[:, 3:4], parts[:, 1:3]], axis=1)
    return parts.transpose(4, 1, 3, 2, 5, 0, 6).reshape(2, 2, 8, 8, 16, 256)


def by_row(columns):
    parts = columns.reshape(2, 4, 2, 16, 2, 8, 256).transpose(5, 1, 3, 2, 0, 4, 6)
    parts = jnp.concatenate([parts[:, 0:1], parts[:, 2:4], parts[:, 1:2]], axis=1)
    return parts.reshape(1, 4096, 256)


def local(tokens, cotangent, first_factor, second_factor, hidden_weight, output_weight):
    x = tokens[0].reshape(8, 512, 256)
    f = first_factor.reshape(8, 16, 2, 4, 512).transpose(0, 2, 1, 3, 4).reshape(8, 128, 512)
    second = second_factor.reshape(2, 4, 128, 512)
    row = lax.broadcasted_iota(jnp.int32, (256, 256), 0)
    col = lax.broadcasted_iota(jnp.int32, (256, 256), 1)
    to_column = (col == (row % 8) * 32 + row // 8).astype(BF)
    to_row = (col == (row % 32) * 8 + row // 32).astype(BF)
    fm, sp, xp = front(x, f, second, to_column)
    out, fg, sg, wg = back(
        fm, sp, x, xp, by_column(tokens), by_column(cotangent),
        hidden_weight, output_weight, hidden_weight.T, output_weight.T, to_row,
    )
    first_grad = fg.reshape(2, 8, 2, 16, 2, 512).transpose(1, 3, 2, 0, 4, 5).reshape(8, 128, 512)
    wg = wg.reshape(2, 256, 768)
    return by_row(out), first_grad, sg.reshape(8, 128, 512), wg[0], wg[1].T


def solution(mesh):
    in_specs = (
        P("dp", "seq", None),
        P("dp", "seq", None),
        P("seq", "dp", None),
        P("seq", "dp", None),
        P(),
        P(),
    )
    out_specs = (P("dp", "seq", None), P("seq", "dp", None), P("seq", "dp", None), P(), P())
    return jax.shard_map(local, mesh=mesh, in_specs=in_specs, out_specs=out_specs, check_vma=False)
```

```python
import math

import jax
import jax.numpy as jnp
import numpy as np
from jax import lax
from jax.experimental import pallas as pl
from jax.experimental.pallas import tpu as pltpu
from jax.sharding import PartitionSpec as P

MESH = pl.DeviceIdType.MESH
BF = jnp.bfloat16
F32 = jnp.float32
DMA = pltpu.SemaphoreType.DMA
ANY = pl.BlockSpec(memory_space=pl.ANY)
VM = pl.BlockSpec(memory_space=pltpu.VMEM)
BLOCK_SCALE = 1.0 / math.sqrt(1024.0)
WEIGHT_SCALE = 1.0 / math.sqrt(1048576.0)
SINGLES = (
    "lx", "lf", "lc", "f_s", "f_r", "sa_s0", "sa_s1", "sa_r", "sb_s", "sb_r", "x_s0", "x_s1", "x_r0", "x_r1",
    "a1_s", "a1_ra", "a1_rb", "a2_sa", "a2_ra", "a3_sa", "a3_ra", "a4_sa", "a4_ra",
    "go_r", "rs_s", "rs_r", "zl_s", "zl_r", "z_s", "z_r", "ag_s", "ag_r", "t_out", "t_first", "t_hid", "t_wide",
)
FOURS = ("a2_s", "a2_r", "a3_s", "a3_r", "a4_s", "a4_r", "g_s", "g_r", "h_s", "h_r", "go_s0", "go_s1")


def dev(s, p):
    return {"seq": s, "dp": p}


def offset(s, i):
    z, x, y, c = s // 32, (s // 8) % 4, (s // 2) % 4, s % 2
    j = i // 2
    z = (z + i) % 2
    x = (x + j) % 4
    y = (y + j // 4 + j) % 4
    c = (c + j // 16) % 2
    return z * 32 + x * 8 + y * 2 + c


def remote(src, dst, ssem, rsem, s, p):
    return pltpu.make_async_remote_copy(src, dst, ssem, rsem, device_id=dev(s, p), device_id_type=MESH)


def drain(ref, sem):
    pltpu.make_async_copy(ref, ref, sem).wait()


def loop(n, body, start=0):
    def step(i, carry):
        body(i)
        return carry

    lax.fori_loop(start, n, step, 0)


def rows_at(start, n):
    return pl.ds(pl.multiple_of(start, n), n)


def dot(a, b, dims=((1,), (0,))):
    return lax.dot_general(a, b, (dims, ((), ())), preferred_element_type=F32)


def pack(rows):
    tiles = rows.reshape(-1, 8, 256)
    return jnp.concatenate([tiles[:, :, :128], tiles[:, :, 128:]], axis=1).astype(BF)


def unpack(tiles):
    tiles = tiles.reshape(-1, 16, 128).astype(F32)
    return jnp.concatenate([tiles[:, :8], tiles[:, 8:]], axis=2).reshape(-1, 256)


def token_tile(mixed, xf, grads, w1, w2, w1t, w2t):
    gate = xf / (1.0 + jnp.exp(-xf))
    gated = (mixed * gate).astype(BF)
    pre = dot(gated, w1)
    root = math.sqrt(2.0 / math.pi)
    square = pre * pre
    tanh = jnp.tanh(pre * (root + (root * 0.044715) * square))
    half = 0.5 * (1.0 + tanh)
    activated = (pre * half).astype(BF)
    slope = half + 0.5 * pre * (1.0 - tanh * tanh) * (root + (3.0 * root * 0.044715) * square)
    output = gated.astype(F32) + dot(activated, w2)
    low = grads.astype(BF)
    d_hidden = (dot(low, w2t) * slope).astype(BF)
    out_part = dot(low, activated, ((0,), (0,)))
    hid_part = dot(gated, d_hidden, ((0,), (0,)))
    d_mixed = (grads + dot(d_hidden, w1t)) * gate
    return output, d_mixed, hid_part, out_part


def kernel(
    x_ref, c_ref, f_ref, s_ref, w1, w2, to_col, to_row, to_block, to_k,
    out_ref, fg_ref, sg_ref, hid_ref, wide_ref,
    xe, raw, f2, fmx, fs, fm, fmk, sp, st, xt, ct, ob, mb, mr, db, dr, dmk, dfb, dfr, dfa,
    gb, gr, go, fgb, fgr, fgo, acc, rsb, zl, zb, agb, wide, w1t, w2t, single, fours,
):
    one = {name: single.at[n] for n, name in enumerate(SINGLES)}
    four = {name: fours.at[n] for n, name in enumerate(FOURS)}
    s, p = lax.axis_index("seq"), lax.axis_index("dp")
    z, b = s // 32, (s // 16) % 2
    mate, cross = p + 1 - 2 * (p % 2), 3 - p
    twin, flip = s + 16 * (1 - 2 * b), s + 32 * (1 - 2 * z)
    side, odd = p // 2, p % 2
    kind = (p + side) % 2
    same = (z + b) % 2 == kind
    unlike = jnp.logical_not(same)
    base = 2 * side

    load_x = pltpu.make_async_copy(x_ref, xe.at[:, :, 0:256], one["lx"])
    load_f = pltpu.make_async_copy(f_ref, f2.at[:, side], one["lf"])
    load_c = pltpu.make_async_copy(c_ref, raw, one["lc"])
    load_x.start()
    load_f.start()
    load_c.start()

    bar = pltpu.get_barrier_semaphore()

    def greet(t, q):
        pl.semaphore_signal(bar, 1, device_id=dev(t, q), device_id_type=MESH)

    greet(s, mate)
    for q in (2 - base, 3 - base):
        greet(s, q)
        greet(flip, q)

    def hello(i):
        greet(offset(s, i), p)
        greet(offset(s, i), mate)

    loop(64, hello, 1)
    pl.semaphore_wait(bar, 131)

    remote(f_ref, f2.at[:, side], one["f_s"], one["f_r"], s, cross).start()
    dest = jnp.where(same, p, mate)
    remote(s_ref.at[1 - b], sp.at[:, p], one["sa_s0"], one["sa_r"], twin, dest).start()

    @pl.when(same)
    def _():
        pltpu.make_async_copy(s_ref.at[b], sp.at[:, p], one["sa_r"]).start()

    @pl.when(unlike)
    def _():
        remote(s_ref.at[b], sp.at[:, p], one["sa_s1"], one["sa_r"], s, mate).start()

    def x_half(n):
        lanes = slice(128 * n, 128 * n + 128)
        return remote(
            x_ref.at[:, :, lanes], xe.at[:, :, 256 + 128 * n:384 + 128 * n], one[f"x_s{n}"], one[f"x_r{n}"], s, mate
        )

    x_half(0).start()

    w1t[...] = w1[...].T
    w2t[...] = w2[...].T

    def to_columns(src, dst):
        def group(n):
            q, rg = n // 4, n % 4
            rel = (q // 2 + q % 2 + kind) % 2
            rows = src[:, rows_at(n * 32, 32), 0:256].reshape(256, 256)
            tiles = pack(dot(to_col[...], rows)).reshape(2, 4, 4, 16, 128)
            for h in range(2):
                dst[rel, (q // 2) * 4 + h * 2 + rg // 2, pl.ds((rg % 2) * 4, 4)] = tiles[h]

        loop(16, group)

    load_x.wait()
    to_columns(xe, xt)
    load_c.wait()
    to_columns(raw, ct)
    acc[...] = jnp.zeros_like(acc)

    def first_mix(e, lane, width):
        def block(a):
            fmx[a, :, 0:width] = dot(f2[a].reshape(256, 512), xe[a, :, 256 * e + lane:256 * e + lane + width]).astype(BF)

        loop(8, block)

        def group(n):
            q, rg = n // 4, n % 4
            rows = fmx[:, rows_at(n * 32, 32), 0:width].reshape(256, width)
            tiles = dot(to_col[...], rows).astype(BF).reshape(2, 4, 32, width)
            for h in range(2):
                fs[e, pl.ds(q * 32 + h * 16 + rg * 4, 4), :, lane:lane + width] = tiles[h]

        loop(8, group)
        lanes = slice(lane, lane + width)
        rsem = one["a1_rb" if e else "a1_ra"]
        pltpu.make_async_copy(fs.at[e, s, :, lanes], fm.at[e, s, :, lanes], rsem).start()

        def send(i):
            t = offset(s, i)
            remote(fs.at[e, t, :, lanes], fm.at[e, s, :, lanes], one["a1_s"], rsem, t, p).start()

        loop(64, send, 1)

    load_f.wait()
    drain(f2.at[:, 1 - side], one["f_r"])
    first_mix(0, 0, 256)
    drain(sp.at[:, pl.ds(0, 2)], one["sa_r"])
    half = sp.at[:, pl.ds(base, 2)]
    remote(half, half, one["sb_s"], one["sb_r"], s, cross).start()
    x_half(0).wait_send()
    x_half(1).start()
    x_half(0).wait_recv()
    first_mix(1, 0, 128)

    def mixed_columns(e):
        def piece(t):
            rows = fm[e, pl.ds(t * 16, 16)].astype(F32)
            for k in range(4):
                fmk[k, rows_at(t * 128, 128), 256 * e:256 * e + 256] = (
                    rows[:, 8 * k:8 * k + 8, :].reshape(128, 256).astype(BF)
                )

        loop(4, piece)

    def second_mix(e, k):
        def piece(t):
            mb[e, pl.ds(t * 16, 16), k] = pack(dot(sp[k, t], fmk[k, :, 256 * e:256 * e + 256]))

        loop(4, piece)

    drain(sp.at[:, pl.ds(0, 2)], one["sb_r"])
    drain(fs.at[0], one["a1_ra"])
    mixed_columns(0)
    for k in range(4):
        second_mix(0, k)
    pltpu.make_async_copy(mb.at[0, s], mr.at[0, s // 8, s % 8], one["a2_ra"]).start()

    def send_own(i):
        t = offset(s, i)
        remote(mb.at[0, t], mr.at[0, s // 8, s % 8], one["a2_sa"], one["a2_ra"], t, p).start()

    loop(64, send_own, 1)

    def turn_second(k):
        for t in range(4):
            for u in range(4):
                st[k, u, :, 128 * t:128 * t + 128] = sp[k, t, :, 128 * u:128 * u + 128].T

    loop(4, turn_second)

    x_half(1).wait_recv()
    first_mix(1, 128, 128)

    def tokens(rel, pick, shape):
        output, d_mixed, hid_part, out_part = token_tile(
            unpack(pick(mr)[...]), unpack(pick(xt)[...]), unpack(pick(ct)[...]), w1[...], w2[...], w1t[...], w2t[...]
        )
        pick(ob)[...] = pack(output).reshape(shape)
        pick(db)[...] = pack(d_mixed).reshape(shape)
        acc[0:16] += hid_part.reshape(16, 16, 768)
        acc[16:32] += out_part.reshape(16, 16, 768)

    drain(mb.at[0], one["a2_ra"])

    def own_tile(n):
        lo = (s + n) % 8
        tokens(0, lambda ref: ref.at[0, :, lo], (8, 4, 16, 128))

        def send(m):
            hi = (s // 8 + m) % 8
            t = hi * 8 + lo
            here = t == s

            @pl.when(here)
            def _():
                pltpu.make_async_copy(db.at[0, hi, lo], dr.at[0, s], one["a3_ra"]).start()

            @pl.when(jnp.logical_not(here))
            def _():
                remote(db.at[0, hi, lo], dr.at[0, s], one["a3_sa"], one["a3_ra"], t, p).start()

        loop(8, send)

    loop(4, own_tile)

    drain(fs.at[1], one["a1_rb"])
    mixed_columns(1)

    def mate_mix(k):
        second_mix(1, k)

        def send(i):
            t = offset(s, i)
            remote(mb.at[1, t, k], mr.at[1, s // 8, s % 8, k], four["a2_s"].at[k], four["a2_r"].at[k], t, mate).start()

        loop(64, send)

    for k in range(4):
        mate_mix(k)
    loop(8, own_tile, 4)

    def d_columns(e, k):
        def piece(t):
            dmk[k, rows_at(t * 128, 128), 256 * e:256 * e + 256] = unpack(dr[e, pl.ds(t * 16, 16), k]).astype(BF)

        loop(4, piece)

    def first_back(e, k):
        def piece(t):
            dfb[e, pl.ds(t * 16, 16), k] = pack(dot(st[k, t], dmk[k, :, 256 * e:256 * e + 256]))

        loop(4, piece)

    def own_back():
        drain(mb.at[0], one["a3_ra"])
        for k in range(4):
            d_columns(0, k)
            first_back(0, k)
        pltpu.make_async_copy(dfb.at[0, s], dfr.at[0, s], one["a4_ra"]).start()

        def send(i):
            t = offset(s, i)
            remote(dfb.at[0, t], dfr.at[0, s], one["a4_sa"], one["a4_ra"], t, p).start()

        loop(64, send, 1)

    def mate_tokens(k):
        drain(mb.at[1, :, k], four["a2_r"].at[k])

        def tile(n):
            lo = 4 * ((s // 4 + n) % 2)
            tokens(1, lambda ref: ref.at[1, :, pl.ds(lo, 4), k], (8, 4, 16, 128))

            def send(m):
                t = ((s // 8 + m) % 8) * 8 + lo + (s + m // 8) % 4
                remote(
                    db.at[1, t // 8, t % 8, k], dr.at[1, s, k], four["a3_s"].at[k], four["a3_r"].at[k], t, mate
                ).start()

            loop(32, send)

        loop(2, tile)

    def mate_back(k):
        drain(mb.at[1, :, k], four["a3_r"].at[k])
        d_columns(1, k)

        def piece(t):
            gb[k, t] = dot(dmk[k, rows_at(t * 128, 128), :], fmk[k], ((1,), (1,))).astype(BF)

        loop(4, piece)
        remote(gb.at[k, pl.ds(2 - base, 2)], gr.at[k], four["g_s"].at[k], four["g_r"].at[k], s, cross).start()
        first_back(1, k)
        pltpu.make_async_copy(dfb.at[1, s, k], dfr.at[1, s, k], four["a4_r"].at[k]).start()

        def send(i):
            t = offset(s, i)
            remote(dfb.at[1, t, k], dfr.at[1, s, k], four["a4_s"].at[k], four["a4_r"].at[k], t, p).start()

        loop(64, send, 1)

    def first_grad(k):
        drain(dfb.at[1, :, k], four["a4_r"].at[k])
        for e in range(2):
            for g in range(2):
                rows = unpack(dfr[e, 32 * g:32 * g + 32, k]).astype(BF)
                dfa[:, 32 * g:32 * g + 32, 256 * e:256 * e + 256] = (
                    dot(to_block[...], rows).astype(BF).reshape(8, 32, 256)
                )

        def block(a):
            fgb[k, :, a] = dot(dfa[a], xe[a], ((1,), (1,))).astype(BF).reshape(2, 32, 512)

        loop(8, block)
        remote(fgb.at[k, 1 - side], fgr.at[k], four["h_s"].at[k], four["h_r"].at[k], s, cross).start()

    def second_sum(k):
        drain(gr.at[k], four["g_r"].at[k])
        mine = gb[k, pl.ds(base, 2)].astype(F32)
        go[k] = ((mine + gr[k].astype(F32)) * BLOCK_SCALE).astype(BF)
        home = jnp.where(same, s, twin)
        remote(go.at[k, 1 - odd], sg_ref.at[4 * b + k], four["go_s0"].at[k], one["go_r"], home, mate).start()

        @pl.when(same)
        def _():
            pltpu.make_async_copy(go.at[k, odd], sg_ref.at[4 * b + k], one["go_r"]).start()

        @pl.when(unlike)
        def _():
            remote(go.at[k, odd], sg_ref.at[4 * b + k], four["go_s1"].at[k], one["go_r"], twin, p).start()

    w = s % 32

    def reduce_start():
        pltpu.make_async_copy(acc.at[w], rsb.at[w], one["rs_r"]).start()

        def send(i):
            t = (w + i) % 32
            remote(acc.at[t], rsb.at[w], one["rs_s"], one["rs_r"], z * 32 + t, p).start()

        loop(32, send, 1)

    def reduce_pair():
        drain(rsb, one["rs_r"])
        zl[0] = jnp.sum(rsb[...], axis=0)
        remote(zl.at[0], zl.at[1], one["zl_s"], one["zl_r"], flip, p).start()

    def reduce_planes():
        drain(zl.at[1], one["zl_r"])
        zb[p] = zl[0] + zl[1]
        for i in range(1, 4):
            remote(zb.at[p], zb.at[p], one["z_s"], one["z_r"], s, (p + i) % 4).start()

    def reduce_gather():
        drain(zb.at[pl.ds(0, 3)], one["z_r"])
        agb[w] = jnp.sum(zb[...], axis=0) * WEIGHT_SCALE

        def send(i):
            remote(agb.at[w], agb.at[w], one["ag_s"], one["ag_r"], z * 32 + (w + i) % 32, p).start()

        loop(32, send, 1)

    own_back()
    mate_tokens(0)
    mate_tokens(1)
    mate_back(0)
    mate_tokens(2)
    mate_back(1)
    drain(dfb.at[0], one["a4_ra"])
    first_grad(0)
    mate_tokens(3)
    reduce_start()
    mate_back(2)
    first_grad(1)
    second_sum(0)
    mate_back(3)
    reduce_pair()
    first_grad(2)
    second_sum(1)
    reduce_planes()
    first_grad(3)
    second_sum(2)
    reduce_gather()

    def to_rows(n):
        q, rg = n // 4, n % 4
        rel = (q // 2 + q % 2 + kind) % 2
        lo = (rg % 2) * 4
        hi = (q // 2) * 4 + rg // 2
        tiles = jnp.concatenate([ob[rel, hi, pl.ds(lo, 4)], ob[rel, hi + 2, pl.ds(lo, 4)]], axis=0)
        rows = dot(to_row[...], unpack(tiles).astype(BF)).astype(BF)
        raw[:, rows_at(n * 32, 32), :] = rows.reshape(8, 32, 256)

    loop(16, to_rows)
    for n in range(8):
        pltpu.make_async_copy(raw.at[n], out_ref.at[0, pl.ds(512 * n, 512)], one["t_out"]).start()

    second_sum(3)
    drain(agb.at[pl.ds(0, 31)], one["ag_r"])
    pltpu.make_async_copy(agb.at[pl.ds(0, 16)], hid_ref, one["t_hid"]).start()
    for n in range(6):
        wide[128 * n:128 * n + 128, :] = agb[16:32, :, 128 * n:128 * n + 128].reshape(256, 128).T
    pltpu.make_async_copy(wide, wide_ref, one["t_wide"]).start()

    for k in range(4):
        drain(fgr.at[k], four["h_r"].at[k])

    def first_sum(a):
        total = (fgb[:, side, a].astype(F32) + fgr[:, a].astype(F32)) * BLOCK_SCALE
        fgo[a] = dot(to_k[...], total.astype(BF).reshape(128, 512)).astype(BF)

    loop(8, first_sum)
    pltpu.make_async_copy(fgo, fg_ref, one["t_first"]).start()

    drain(f_ref, one["f_s"])
    drain(s_ref.at[0], one["sa_s0"])

    @pl.when(unlike)
    def _():
        drain(s_ref.at[0], one["sa_s1"])
        for k in range(4):
            drain(go.at[k, 0], four["go_s1"].at[k])

    drain(half, one["sb_s"])
    x_half(1).wait_send()
    drain(fs.at[:, pl.ds(0, 63)], one["a1_s"])
    for name in ("a2_sa", "a3_sa", "a4_sa"):
        drain(mb.at[0, pl.ds(0, 63)], one[name])
    for k in range(4):
        drain(mb.at[1, :, k], four["a2_s"].at[k])
        drain(mb.at[1, :, k], four["a3_s"].at[k])
        drain(mb.at[1, pl.ds(0, 63), k], four["a4_s"].at[k])
        drain(gr.at[k], four["g_s"].at[k])
        drain(fgr.at[k], four["h_s"].at[k])
        drain(go.at[k, 0], four["go_s0"].at[k])
    drain(rsb.at[pl.ds(0, 31)], one["rs_s"])
    drain(zl.at[0], one["zl_s"])
    drain(zb.at[pl.ds(0, 3)], one["z_s"])
    drain(agb.at[pl.ds(0, 31)], one["ag_s"])
    drain(sg_ref, one["go_r"])
    drain(raw, one["t_out"])
    drain(fgo, one["t_first"])
    drain(agb.at[pl.ds(0, 16)], one["t_hid"])
    drain(wide, one["t_wide"])


def permutation(*shape_and_order):
    shape, order = shape_and_order
    places = np.arange(math.prod(shape)).reshape(shape).transpose(order).reshape(-1)
    return np.eye(places.size, dtype=np.float32)[places]


def local(tokens, cotangent, first_factor, second_factor, hidden_weight, output_weight):
    to_col = permutation((8, 4, 2, 4), (2, 1, 3, 0))
    to_block = permutation((32, 8), (1, 0))
    to_k = permutation((4, 2, 16), (2, 1, 0))
    tiles = (2, 8, 8, 4, 16, 128)
    pieces = (2, 64, 4, 16, 128)
    scratch = [
        ((8, 512, 512), BF), ((8, 512, 256), BF), ((8, 2, 128, 512), BF), ((8, 256, 256), BF),
        ((2, 64, 32, 256), BF), ((2, 64, 32, 256), BF), ((4, 512, 512), BF),
        ((4, 4, 128, 512), BF), ((4, 4, 128, 512), BF),
        (tiles, BF), (tiles, BF), (tiles, BF), (pieces, BF), (tiles, BF), (tiles, BF), (pieces, BF),
        ((4, 512, 512), BF), (pieces, BF), (pieces, BF), ((8, 64, 512), BF),
        ((4, 4, 128, 512), BF), ((4, 2, 128, 512), BF), ((4, 2, 128, 512), BF),
        ((4, 2, 8, 32, 512), BF), ((4, 8, 32, 512), BF), ((8, 128, 512), BF),
        ((32, 16, 768), F32), ((32, 16, 768), F32), ((2, 16, 768), F32), ((4, 16, 768), F32), ((32, 16, 768), F32),
        ((768, 256), F32), ((768, 256), BF), ((256, 768), BF),
    ]
    out, fg, sg, hid, wide = pl.pallas_call(
        kernel,
        out_shape=(
            jax.ShapeDtypeStruct((1, 4096, 256), BF),
            jax.ShapeDtypeStruct((8, 128, 512), BF),
            jax.ShapeDtypeStruct((8, 128, 512), BF),
            jax.ShapeDtypeStruct((16, 16, 768), F32),
            jax.ShapeDtypeStruct((768, 256), F32),
        ),
        in_specs=[ANY] * 4 + [VM] * 6,
        out_specs=(ANY,) * 5,
        scratch_shapes=[pltpu.VMEM(*shape) for shape in scratch]
        + [DMA((len(SINGLES),)), DMA((len(FOURS), 4))],
        compiler_params=pltpu.CompilerParams(
            collective_id=1, has_side_effects=True, vmem_limit_bytes=62 << 20
        ),
    )(
        tokens.reshape(8, 512, 256), cotangent.reshape(8, 512, 256), first_factor,
        second_factor.reshape(2, 4, 128, 512), hidden_weight, output_weight,
        jnp.asarray(to_col, BF), jnp.asarray(to_col.T, BF), jnp.asarray(to_block, BF), jnp.asarray(to_k, BF),
    )
    return out, fg, sg, hid.reshape(256, 768), wide


def solution(mesh):
    in_specs = (
        P("dp", "seq", None),
        P("dp", "seq", None),
        P("seq", "dp", None),
        P("seq", "dp", None),
        P(),
        P(),
    )
    out_specs = (P("dp", "seq", None), P("seq", "dp", None), P("seq", "dp", None), P(), P())
    return jax.shard_map(local, mesh=mesh, in_specs=in_specs, out_specs=out_specs, check_vma=False)
```

```python
import math

import jax
import jax.numpy as jnp
import numpy as np
from jax import lax
from jax.experimental import pallas as pl
from jax.experimental.pallas import tpu as pltpu
from jax.sharding import PartitionSpec as P

MESH = pl.DeviceIdType.MESH
BF = jnp.bfloat16
F32 = jnp.float32
DMA = pltpu.SemaphoreType.DMA
ANY = pl.BlockSpec(memory_space=pl.ANY)
VM = pl.BlockSpec(memory_space=pltpu.VMEM)
BLOCK_SCALE = 1.0 / math.sqrt(1024.0)
WEIGHT_SCALE = 1.0 / math.sqrt(1048576.0)
SINGLES = (
    "lx", "lf", "lc", "f_s", "f_r", "sa_s0", "sa_s1", "sa_r", "sb_s", "sb_r", "x_s0", "x_s1", "x_r0", "x_r1",
    "a1_s", "a1_ra", "a1_rb", "a2_sa", "a2_ra", "a3_sa", "a3_ra", "a4_sa", "a4_ra",
    "go_r", "rs_s", "rs_r", "zl_s", "zl_r", "z_s", "z_r", "ag_s", "ag_r", "t_out", "t_first", "t_hid", "t_wide",
)
FOURS = ("a2_s", "a2_r", "a3_s", "a3_r", "a4_s", "a4_r", "g_s", "g_r", "h_s", "h_r", "go_s0", "go_s1")


def dev(s, p):
    return {"seq": s, "dp": p}


def offset(s, i):
    z, x, y, c = s // 32, (s // 8) % 4, (s // 2) % 4, s % 2
    j = i // 2
    z = (z + i) % 2
    x = (x + j) % 4
    y = (y + j // 4 + j) % 4
    c = (c + j // 16) % 2
    return z * 32 + x * 8 + y * 2 + c


def remote(src, dst, ssem, rsem, s, p):
    return pltpu.make_async_remote_copy(src, dst, ssem, rsem, device_id=dev(s, p), device_id_type=MESH)


def drain(ref, sem):
    pltpu.make_async_copy(ref, ref, sem).wait()


def loop(n, body, start=0):
    def step(i, carry):
        body(i)
        return carry

    lax.fori_loop(start, n, step, 0)


def rows_at(start, n):
    return pl.ds(pl.multiple_of(start, n), n)


def dot(a, b, dims=((1,), (0,))):
    return lax.dot_general(a, b, (dims, ((), ())), preferred_element_type=F32)


def pack(rows):
    tiles = rows.reshape(-1, 8, 256)
    return jnp.concatenate([tiles[:, :, :128], tiles[:, :, 128:]], axis=1).astype(BF)


def unpack(tiles):
    tiles = tiles.reshape(-1, 16, 128).astype(F32)
    return jnp.concatenate([tiles[:, :8], tiles[:, 8:]], axis=2).reshape(-1, 256)


def token_tile(mixed, xf, grads, w1, w2, w1t, w2t):
    gate = xf / (1.0 + jnp.exp(-xf))
    gated = (mixed * gate).astype(BF)
    pre = dot(gated, w1)
    root = math.sqrt(2.0 / math.pi)
    square = pre * pre
    tanh = jnp.tanh(pre * (root + (root * 0.044715) * square))
    half = 0.5 * (1.0 + tanh)
    activated = (pre * half).astype(BF)
    slope = half + 0.5 * pre * (1.0 - tanh * tanh) * (root + (3.0 * root * 0.044715) * square)
    output = gated.astype(F32) + dot(activated, w2)
    low = grads.astype(BF)
    d_hidden = (dot(low, w2t) * slope).astype(BF)
    out_part = dot(low, activated, ((0,), (0,)))
    hid_part = dot(gated, d_hidden, ((0,), (0,)))
    d_mixed = (grads + dot(d_hidden, w1t)) * gate
    return output, d_mixed, hid_part, out_part


def kernel(
    x_ref, c_ref, f_ref, s_ref, w1, w2, to_col, to_row, to_block, to_k,
    out_ref, fg_ref, sg_ref, hid_ref, wide_ref,
    xe, raw, f2, fmx, fs, fm, fmk, sp, st, xt, ct, ob, mb, mr, db, dr, dmk, dfb, dfr, dfa,
    gb, gr, go, fgb, fgr, fgo, acc, rsb, zl, zb, agb, wide, w1t, w2t, single, fours,
):
    one = {name: single.at[n] for n, name in enumerate(SINGLES)}
    four = {name: fours.at[n] for n, name in enumerate(FOURS)}
    s, p = lax.axis_index("seq"), lax.axis_index("dp")
    z, b = s // 32, (s // 16) % 2
    mate, cross = p + 1 - 2 * (p % 2), 3 - p
    twin, flip = s + 16 * (1 - 2 * b), s + 32 * (1 - 2 * z)
    side, odd = p // 2, p % 2
    kind = (p + side) % 2
    same = (z + b) % 2 == kind
    unlike = jnp.logical_not(same)
    base = 2 * side

    load_x = pltpu.make_async_copy(x_ref, xe.at[:, :, 0:256], one["lx"])
    load_f = pltpu.make_async_copy(f_ref, f2.at[:, side], one["lf"])
    load_c = pltpu.make_async_copy(c_ref, raw, one["lc"])
    load_x.start()
    load_f.start()
    load_c.start()

    bar = pltpu.get_barrier_semaphore()

    def greet(t, q):
        pl.semaphore_signal(bar, 1, device_id=dev(t, q), device_id_type=MESH)

    greet(s, mate)
    for q in (2 - base, 3 - base):
        greet(s, q)
        greet(flip, q)

    def hello(i):
        greet(offset(s, i), p)
        greet(offset(s, i), mate)

    loop(64, hello, 1)
    pl.semaphore_wait(bar, 131)

    remote(f_ref, f2.at[:, side], one["f_s"], one["f_r"], s, cross).start()
    dest = jnp.where(same, p, mate)
    remote(s_ref.at[1 - b], sp.at[:, p], one["sa_s0"], one["sa_r"], twin, dest).start()

    @pl.when(same)
    def _():
        pltpu.make_async_copy(s_ref.at[b], sp.at[:, p], one["sa_r"]).start()

    @pl.when(unlike)
    def _():
        remote(s_ref.at[b], sp.at[:, p], one["sa_s1"], one["sa_r"], s, mate).start()

    def x_half(n):
        lanes = slice(128 * n, 128 * n + 128)
        return remote(
            x_ref.at[:, :, lanes], xe.at[:, :, 256 + 128 * n:384 + 128 * n], one[f"x_s{n}"], one[f"x_r{n}"], s, mate
        )

    x_half(0).start()

    w1t[...] = w1[...].T
    w2t[...] = w2[...].T

    def to_columns(src, dst):
        def group(n):
            q, rg = n // 4, n % 4
            rel = (q // 2 + q % 2 + kind) % 2
            rows = src[:, rows_at(n * 32, 32), 0:256].reshape(256, 256)
            tiles = pack(dot(to_col[...], rows)).reshape(2, 4, 4, 16, 128)
            for h in range(2):
                dst[rel, (q // 2) * 4 + h * 2 + rg // 2, pl.ds((rg % 2) * 4, 4)] = tiles[h]

        loop(16, group)

    load_x.wait()
    to_columns(xe, xt)
    load_c.wait()
    to_columns(raw, ct)
    acc[...] = jnp.zeros_like(acc)

    def first_mix(e, lane, width):
        def block(a):
            fmx[a, :, 0:width] = dot(f2[a].reshape(256, 512), xe[a, :, 256 * e + lane:256 * e + lane + width]).astype(BF)

        loop(8, block)

        def group(n):
            q, rg = n // 4, n % 4
            rows = fmx[:, rows_at(n * 32, 32), 0:width].reshape(256, width)
            tiles = dot(to_col[...], rows).astype(BF).reshape(2, 4, 32, width)
            for h in range(2):
                fs[e, pl.ds(q * 32 + h * 16 + rg * 4, 4), :, lane:lane + width] = tiles[h]

        loop(8, group)
        lanes = slice(lane, lane + width)
        rsem = one["a1_rb" if e else "a1_ra"]
        pltpu.make_async_copy(fs.at[e, s, :, lanes], fm.at[e, s, :, lanes], rsem).start()

        def send(i):
            t = offset(s, i)
            remote(fs.at[e, t, :, lanes], fm.at[e, s, :, lanes], one["a1_s"], rsem, t, p).start()

        loop(64, send, 1)

    load_f.wait()
    drain(f2.at[:, 1 - side], one["f_r"])
    first_mix(0, 0, 256)
    drain(sp.at[:, pl.ds(0, 2)], one["sa_r"])
    half = sp.at[:, pl.ds(base, 2)]
    remote(half, half, one["sb_s"], one["sb_r"], s, cross).start()
    x_half(0).wait_send()
    x_half(1).start()
    x_half(0).wait_recv()
    first_mix(1, 0, 128)

    def mixed_columns(e):
        def piece(t):
            rows = fm[e, pl.ds(t * 16, 16)].astype(F32)
            for k in range(4):
                fmk[k, rows_at(t * 128, 128), 256 * e:256 * e + 256] = (
                    rows[:, 8 * k:8 * k + 8, :].reshape(128, 256).astype(BF)
                )

        loop(4, piece)

    def second_mix(e, k):
        def piece(t):
            mb[e, pl.ds(t * 16, 16), k] = pack(dot(sp[k, t], fmk[k, :, 256 * e:256 * e + 256]))

        loop(4, piece)

    drain(sp.at[:, pl.ds(0, 2)], one["sb_r"])
    drain(fs.at[0], one["a1_ra"])
    mixed_columns(0)
    for k in range(4):
        second_mix(0, k)
    pltpu.make_async_copy(mb.at[0, s], mr.at[0, s // 8, s % 8], one["a2_ra"]).start()

    def send_own(i):
        t = offset(s, i)
        remote(mb.at[0, t], mr.at[0, s // 8, s % 8], one["a2_sa"], one["a2_ra"], t, p).start()

    loop(64, send_own, 1)

    def turn_second(k):
        for t in range(4):
            for u in range(4):
                st[k, u, :, 128 * t:128 * t + 128] = sp[k, t, :, 128 * u:128 * u + 128].T

    loop(4, turn_second)

    x_half(1).wait_recv()
    first_mix(1, 128, 128)

    def tokens(rel, pick, shape):
        output, d_mixed, hid_part, out_part = token_tile(
            unpack(pick(mr)[...]), unpack(pick(xt)[...]), unpack(pick(ct)[...]), w1[...], w2[...], w1t[...], w2t[...]
        )
        pick(ob)[...] = pack(output).reshape(shape)
        pick(db)[...] = pack(d_mixed).reshape(shape)
        acc[0:16] += hid_part.reshape(16, 16, 768)
        acc[16:32] += out_part.reshape(16, 16, 768)

    drain(mb.at[0], one["a2_ra"])

    def own_tile(n):
        lo = (s + n) % 8
        tokens(0, lambda ref: ref.at[0, :, lo], (8, 4, 16, 128))

        def send(m):
            hi = (s // 8 + m) % 8
            t = hi * 8 + lo
            here = t == s

            @pl.when(here)
            def _():
                pltpu.make_async_copy(db.at[0, hi, lo], dr.at[0, s], one["a3_ra"]).start()

            @pl.when(jnp.logical_not(here))
            def _():
                remote(db.at[0, hi, lo], dr.at[0, s], one["a3_sa"], one["a3_ra"], t, p).start()

        loop(8, send)

    loop(4, own_tile)

    drain(fs.at[1], one["a1_rb"])
    mixed_columns(1)

    def mate_mix(k):
        second_mix(1, k)

        def send(i):
            t = offset(s, i)
            remote(mb.at[1, t, k], mr.at[1, s // 8, s % 8, k], four["a2_s"].at[k], four["a2_r"].at[k], t, mate).start()

        loop(64, send)

    for k in range(3):
        mate_mix(k)
    loop(8, own_tile, 4)

    def d_columns(e, k):
        def piece(t):
            dmk[k, rows_at(t * 128, 128), 256 * e:256 * e + 256] = unpack(dr[e, pl.ds(t * 16, 16), k]).astype(BF)

        loop(4, piece)

    def first_back(e, k):
        def piece(t):
            dfb[e, pl.ds(t * 16, 16), k] = pack(dot(st[k, t], dmk[k, :, 256 * e:256 * e + 256]))

        loop(4, piece)

    def own_back():
        drain(mb.at[0], one["a3_ra"])
        for k in range(4):
            d_columns(0, k)
            first_back(0, k)
        pltpu.make_async_copy(dfb.at[0, s], dfr.at[0, s], one["a4_ra"]).start()

        def send(i):
            t = offset(s, i)
            remote(dfb.at[0, t], dfr.at[0, s], one["a4_sa"], one["a4_ra"], t, p).start()

        loop(64, send, 1)

    def mate_tokens(k):
        drain(mb.at[1, :, k], four["a2_r"].at[k])

        def tile(n):
            lo = 4 * ((s // 4 + n) % 2)
            tokens(1, lambda ref: ref.at[1, :, pl.ds(lo, 4), k], (8, 4, 16, 128))

            def send(m):
                t = ((s // 8 + m) % 8) * 8 + lo + (s + m // 8) % 4
                remote(
                    db.at[1, t // 8, t % 8, k], dr.at[1, s, k], four["a3_s"].at[k], four["a3_r"].at[k], t, mate
                ).start()

            loop(32, send)

        loop(2, tile)

    def mate_back(k):
        drain(mb.at[1, :, k], four["a3_r"].at[k])
        d_columns(1, k)

        def piece(i):
            t = (2 - base + i) % 4
            gb[k, t] = dot(dmk[k, rows_at(t * 128, 128), :], fmk[k], ((1,), (1,))).astype(BF)

        loop(2, piece)
        remote(gb.at[k, pl.ds(2 - base, 2)], gr.at[k], four["g_s"].at[k], four["g_r"].at[k], s, cross).start()
        first_back(1, k)
        pltpu.make_async_copy(dfb.at[1, s, k], dfr.at[1, s, k], four["a4_r"].at[k]).start()

        def send(i):
            t = offset(s, i)
            remote(dfb.at[1, t, k], dfr.at[1, s, k], four["a4_s"].at[k], four["a4_r"].at[k], t, p).start()

        loop(64, send, 1)
        loop(4, piece, 2)

    def first_grad(k):
        drain(dfb.at[1, :, k], four["a4_r"].at[k])
        for e in range(2):
            for g in range(2):
                rows = unpack(dfr[e, 32 * g:32 * g + 32, k]).astype(BF)
                dfa[:, 32 * g:32 * g + 32, 256 * e:256 * e + 256] = (
                    dot(to_block[...], rows).astype(BF).reshape(8, 32, 256)
                )

        def block(a):
            fgb[k, :, a] = dot(dfa[a], xe[a], ((1,), (1,))).astype(BF).reshape(2, 32, 512)

        for part in (0, 4):
            loop(part + 4, block, part)
            away = fgb.at[k, 1 - side, pl.ds(part, 4)]
            remote(away, fgr.at[k, pl.ds(part, 4)], four["h_s"].at[k], four["h_r"].at[k], s, cross).start()

    def second_sum(k):
        drain(gr.at[k], four["g_r"].at[k])
        mine = gb[k, pl.ds(base, 2)].astype(F32)
        go[k] = ((mine + gr[k].astype(F32)) * BLOCK_SCALE).astype(BF)
        home = jnp.where(same, s, twin)
        remote(go.at[k, 1 - odd], sg_ref.at[4 * b + k], four["go_s0"].at[k], one["go_r"], home, mate).start()

        @pl.when(same)
        def _():
            pltpu.make_async_copy(go.at[k, odd], sg_ref.at[4 * b + k], one["go_r"]).start()

        @pl.when(unlike)
        def _():
            remote(go.at[k, odd], sg_ref.at[4 * b + k], four["go_s1"].at[k], one["go_r"], twin, p).start()

    w = s % 32

    def reduce_start():
        pltpu.make_async_copy(acc.at[w], rsb.at[w], one["rs_r"]).start()

        def send(i):
            t = (w + i) % 32
            remote(acc.at[t], rsb.at[w], one["rs_s"], one["rs_r"], z * 32 + t, p).start()

        loop(32, send, 1)

    def reduce_pair():
        drain(rsb, one["rs_r"])
        zl[0] = jnp.sum(rsb[...], axis=0)
        remote(zl.at[0], zl.at[1], one["zl_s"], one["zl_r"], flip, p).start()

    def reduce_planes():
        drain(zl.at[1], one["zl_r"])
        zb[p] = zl[0] + zl[1]
        for i in range(1, 4):
            remote(zb.at[p], zb.at[p], one["z_s"], one["z_r"], s, (p + i) % 4).start()

    def reduce_gather():
        drain(zb.at[pl.ds(0, 3)], one["z_r"])
        agb[w] = jnp.sum(zb[...], axis=0) * WEIGHT_SCALE

        def send(i):
            remote(agb.at[w], agb.at[w], one["ag_s"], one["ag_r"], z * 32 + (w + i) % 32, p).start()

        loop(32, send, 1)

    own_back()
    mate_tokens(0)
    mate_mix(3)
    mate_tokens(1)
    mate_back(0)
    mate_tokens(2)
    mate_back(1)
    drain(dfb.at[0], one["a4_ra"])
    first_grad(0)
    mate_tokens(3)
    reduce_start()
    mate_back(2)
    first_grad(1)
    second_sum(0)
    mate_back(3)
    reduce_pair()
    first_grad(2)
    second_sum(1)
    reduce_planes()
    first_grad(3)
    second_sum(2)
    reduce_gather()

    def to_rows(n):
        q, rg = n // 4, n % 4
        rel = (q // 2 + q % 2 + kind) % 2
        lo = (rg % 2) * 4
        hi = (q // 2) * 4 + rg // 2
        tiles = jnp.concatenate([ob[rel, hi, pl.ds(lo, 4)], ob[rel, hi + 2, pl.ds(lo, 4)]], axis=0)
        rows = dot(to_row[...], unpack(tiles).astype(BF)).astype(BF)
        raw[:, rows_at(n * 32, 32), :] = rows.reshape(8, 32, 256)

    loop(16, to_rows)
    for n in range(8):
        pltpu.make_async_copy(raw.at[n], out_ref.at[0, pl.ds(512 * n, 512)], one["t_out"]).start()

    second_sum(3)
    drain(agb.at[pl.ds(0, 31)], one["ag_r"])
    pltpu.make_async_copy(agb.at[pl.ds(0, 16)], hid_ref, one["t_hid"]).start()
    for n in range(6):
        wide[128 * n:128 * n + 128, :] = agb[16:32, :, 128 * n:128 * n + 128].reshape(256, 128).T
    pltpu.make_async_copy(wide, wide_ref, one["t_wide"]).start()

    for k in range(4):
        drain(fgr.at[k], four["h_r"].at[k])

    def first_sum(a):
        total = (fgb[:, side, a].astype(F32) + fgr[:, a].astype(F32)) * BLOCK_SCALE
        fgo[a] = dot(to_k[...], total.astype(BF).reshape(128, 512)).astype(BF)

    loop(8, first_sum)
    pltpu.make_async_copy(fgo, fg_ref, one["t_first"]).start()

    drain(f_ref, one["f_s"])
    drain(s_ref.at[0], one["sa_s0"])

    @pl.when(unlike)
    def _():
        drain(s_ref.at[0], one["sa_s1"])
        for k in range(4):
            drain(go.at[k, 0], four["go_s1"].at[k])

    drain(half, one["sb_s"])
    x_half(1).wait_send()
    drain(fs.at[:, pl.ds(0, 63)], one["a1_s"])
    for name in ("a2_sa", "a3_sa", "a4_sa"):
        drain(mb.at[0, pl.ds(0, 63)], one[name])
    for k in range(4):
        drain(mb.at[1, :, k], four["a2_s"].at[k])
        drain(mb.at[1, :, k], four["a3_s"].at[k])
        drain(mb.at[1, pl.ds(0, 63), k], four["a4_s"].at[k])
        drain(gr.at[k], four["g_s"].at[k])
        drain(fgr.at[k], four["h_s"].at[k])
        drain(go.at[k, 0], four["go_s0"].at[k])
    drain(rsb.at[pl.ds(0, 31)], one["rs_s"])
    drain(zl.at[0], one["zl_s"])
    drain(zb.at[pl.ds(0, 3)], one["z_s"])
    drain(agb.at[pl.ds(0, 31)], one["ag_s"])
    drain(sg_ref, one["go_r"])
    drain(raw, one["t_out"])
    drain(fgo, one["t_first"])
    drain(agb.at[pl.ds(0, 16)], one["t_hid"])
    drain(wide, one["t_wide"])


def permutation(*shape_and_order):
    shape, order = shape_and_order
    places = np.arange(math.prod(shape)).reshape(shape).transpose(order).reshape(-1)
    return np.eye(places.size, dtype=np.float32)[places]


def local(tokens, cotangent, first_factor, second_factor, hidden_weight, output_weight):
    to_col = permutation((8, 4, 2, 4), (2, 1, 3, 0))
    to_block = permutation((32, 8), (1, 0))
    to_k = permutation((4, 2, 16), (2, 1, 0))
    tiles = (2, 8, 8, 4, 16, 128)
    pieces = (2, 64, 4, 16, 128)
    scratch = [
        ((8, 512, 512), BF), ((8, 512, 256), BF), ((8, 2, 128, 512), BF), ((8, 256, 256), BF),
        ((2, 64, 32, 256), BF), ((2, 64, 32, 256), BF), ((4, 512, 512), BF),
        ((4, 4, 128, 512), BF), ((4, 4, 128, 512), BF),
        (tiles, BF), (tiles, BF), (tiles, BF), (pieces, BF), (tiles, BF), (tiles, BF), (pieces, BF),
        ((4, 512, 512), BF), (pieces, BF), (pieces, BF), ((8, 64, 512), BF),
        ((4, 4, 128, 512), BF), ((4, 2, 128, 512), BF), ((4, 2, 128, 512), BF),
        ((4, 2, 8, 32, 512), BF), ((4, 8, 32, 512), BF), ((8, 128, 512), BF),
        ((32, 16, 768), F32), ((32, 16, 768), F32), ((2, 16, 768), F32), ((4, 16, 768), F32), ((32, 16, 768), F32),
        ((768, 256), F32), ((768, 256), BF), ((256, 768), BF),
    ]
    out, fg, sg, hid, wide = pl.pallas_call(
        kernel,
        out_shape=(
            jax.ShapeDtypeStruct((1, 4096, 256), BF),
            jax.ShapeDtypeStruct((8, 128, 512), BF),
            jax.ShapeDtypeStruct((8, 128, 512), BF),
            jax.ShapeDtypeStruct((16, 16, 768), F32),
            jax.ShapeDtypeStruct((768, 256), F32),
        ),
        in_specs=[ANY] * 4 + [VM] * 6,
        out_specs=(ANY,) * 5,
        scratch_shapes=[pltpu.VMEM(*shape) for shape in scratch]
        + [DMA((len(SINGLES),)), DMA((len(FOURS), 4))],
        compiler_params=pltpu.CompilerParams(
            collective_id=1, has_side_effects=True, vmem_limit_bytes=62 << 20
        ),
    )(
        tokens.reshape(8, 512, 256), cotangent.reshape(8, 512, 256), first_factor,
        second_factor.reshape(2, 4, 128, 512), hidden_weight, output_weight,
        jnp.asarray(to_col, BF), jnp.asarray(to_col.T, BF), jnp.asarray(to_block, BF), jnp.asarray(to_k, BF),
    )
    return out, fg, sg, hid.reshape(256, 768), wide


def solution(mesh):
    in_specs = (
        P("dp", "seq", None),
        P("dp", "seq", None),
        P("seq", "dp", None),
        P("seq", "dp", None),
        P(),
        P(),
    )
    out_specs = (P("dp", "seq", None), P("seq", "dp", None), P("seq", "dp", None), P(), P())
    return jax.shard_map(local, mesh=mesh, in_specs=in_specs, out_specs=out_specs, check_vma=False)
```

```python
import math

import jax
import jax.numpy as jnp
import numpy as np
from jax import lax
from jax.experimental import pallas as pl
from jax.experimental.pallas import tpu as pltpu
from jax.sharding import PartitionSpec as P

MESH = pl.DeviceIdType.MESH
BF = jnp.bfloat16
F32 = jnp.float32
DMA = pltpu.SemaphoreType.DMA
ANY = pl.BlockSpec(memory_space=pl.ANY)
VM = pl.BlockSpec(memory_space=pltpu.VMEM)
BLOCK_SCALE = 1.0 / math.sqrt(1024.0)
WEIGHT_SCALE = 1.0 / math.sqrt(1048576.0)
SINGLES = (
    "lx", "lf", "lc", "f_s", "f_r", "sa_s0", "sa_s1", "sa_r", "sb_s", "sb_r", "x_s0", "x_s1", "x_r0", "x_r1",
    "a1_s", "a1_ra", "a1_rb", "a2_sa", "a2_ra", "a3_sa", "a3_ra", "a4_sa", "a4_ra",
    "go_r", "rs_s", "rs_r", "zl_s", "zl_r", "z_s", "z_r", "ag_s", "ag_r", "t_out", "t_first", "t_hid", "t_wide",
)
FOURS = ("a2_s", "a2_r", "a3_s", "a3_r", "a4_s", "a4_r", "g_s", "g_r", "h_s", "h_r", "go_s0", "go_s1")


def dev(s, p):
    return {"seq": s, "dp": p}


def offset(s, i):
    z, x, y, c = s // 32, (s // 8) % 4, (s // 2) % 4, s % 2
    j = i // 2
    z = (z + i) % 2
    x = (x + j) % 4
    y = (y + j // 4 + j) % 4
    c = (c + j // 16) % 2
    return z * 32 + x * 8 + y * 2 + c


def remote(src, dst, ssem, rsem, s, p):
    return pltpu.make_async_remote_copy(src, dst, ssem, rsem, device_id=dev(s, p), device_id_type=MESH)


def drain(ref, sem):
    pltpu.make_async_copy(ref, ref, sem).wait()


def loop(n, body, start=0):
    def step(i, carry):
        body(i)
        return carry

    lax.fori_loop(start, n, step, 0)


def rows_at(start, n):
    return pl.ds(pl.multiple_of(start, n), n)


def dot(a, b, dims=((1,), (0,))):
    return lax.dot_general(a, b, (dims, ((), ())), preferred_element_type=F32)


def pack(rows):
    tiles = rows.reshape(-1, 8, 256)
    return jnp.concatenate([tiles[:, :, :128], tiles[:, :, 128:]], axis=1).astype(BF)


def unpack(tiles):
    tiles = tiles.reshape(-1, 16, 128).astype(F32)
    return jnp.concatenate([tiles[:, :8], tiles[:, 8:]], axis=2).reshape(-1, 256)


def token_tile(mixed, xf, grads, w1, w2, w1t, w2t):
    gate = xf / (1.0 + jnp.exp(-xf))
    gated = (mixed * gate).astype(BF)
    pre = dot(gated, w1)
    root = math.sqrt(2.0 / math.pi)
    square = pre * pre
    tanh = jnp.tanh(pre * (root + (root * 0.044715) * square))
    half = 0.5 * (1.0 + tanh)
    activated = (pre * half).astype(BF)
    slope = half + 0.5 * pre * (1.0 - tanh * tanh) * (root + (3.0 * root * 0.044715) * square)
    output = gated.astype(F32) + dot(activated, w2)
    low = grads.astype(BF)
    d_hidden = (dot(low, w2t) * slope).astype(BF)
    out_part = dot(low, activated, ((0,), (0,)))
    hid_part = dot(gated, d_hidden, ((0,), (0,)))
    d_mixed = (grads + dot(d_hidden, w1t)) * gate
    return output, d_mixed, hid_part, out_part


def kernel(
    x_ref, c_ref, f_ref, s_ref, w1, w2, to_col, to_row, to_block, to_k,
    out_ref, fg_ref, sg_ref, hid_ref, wide_ref,
    xe, raw, f2, fmx, fs, fm, fmk, sp, st, xt, ct, ob, mb, mr, db, dr, dmk, dfb, dfr, dfa,
    gb, gr, go, fgb, fgr, fgo, acc, rsb, zl, zb, agb, wide, w1t, w2t, single, fours,
):
    one = {name: single.at[n] for n, name in enumerate(SINGLES)}
    four = {name: fours.at[n] for n, name in enumerate(FOURS)}
    s, p = lax.axis_index("seq"), lax.axis_index("dp")
    z, b = s // 32, (s // 16) % 2
    mate, cross = p + 1 - 2 * (p % 2), 3 - p
    twin, flip = s + 16 * (1 - 2 * b), s + 32 * (1 - 2 * z)
    side, odd = p // 2, p % 2
    kind = (p + side) % 2
    same = (z + b) % 2 == kind
    unlike = jnp.logical_not(same)
    base = 2 * side

    load_x = pltpu.make_async_copy(x_ref, xe.at[:, :, 0:256], one["lx"])
    load_f = pltpu.make_async_copy(f_ref, f2.at[:, side], one["lf"])
    load_c = pltpu.make_async_copy(c_ref, raw, one["lc"])
    load_x.start()
    load_f.start()
    load_c.start()

    bar = pltpu.get_barrier_semaphore()

    def greet(t, q):
        pl.semaphore_signal(bar, 1, device_id=dev(t, q), device_id_type=MESH)

    greet(s, mate)
    for q in (2 - base, 3 - base):
        greet(s, q)
        greet(flip, q)

    def hello(i):
        greet(offset(s, i), p)
        greet(offset(s, i), mate)

    loop(64, hello, 1)
    pl.semaphore_wait(bar, 131)

    remote(f_ref, f2.at[:, side], one["f_s"], one["f_r"], s, cross).start()
    dest = jnp.where(same, p, mate)
    remote(s_ref.at[1 - b], sp.at[:, p], one["sa_s0"], one["sa_r"], twin, dest).start()

    @pl.when(same)
    def _():
        pltpu.make_async_copy(s_ref.at[b], sp.at[:, p], one["sa_r"]).start()

    @pl.when(unlike)
    def _():
        remote(s_ref.at[b], sp.at[:, p], one["sa_s1"], one["sa_r"], s, mate).start()

    def x_half(n):
        lanes = slice(128 * n, 128 * n + 128)
        return remote(
            x_ref.at[:, :, lanes], xe.at[:, :, 256 + 128 * n:384 + 128 * n], one[f"x_s{n}"], one[f"x_r{n}"], s, mate
        )

    x_half(0).start()

    w1t[...] = w1[...].T
    w2t[...] = w2[...].T

    def to_columns(src, dst):
        def group(n):
            q, rg = n // 4, n % 4
            rel = (q // 2 + q % 2 + kind) % 2
            rows = src[:, rows_at(n * 32, 32), 0:256].reshape(256, 256)
            tiles = pack(dot(to_col[...], rows)).reshape(2, 4, 4, 16, 128)
            for h in range(2):
                dst[rel, (q // 2) * 4 + h * 2 + rg // 2, pl.ds((rg % 2) * 4, 4)] = tiles[h]

        loop(16, group)

    load_x.wait()
    to_columns(xe, xt)
    load_c.wait()
    to_columns(raw, ct)
    acc[...] = jnp.zeros_like(acc)

    def first_mix(e, lane, width):
        def block(a):
            fmx[a, :, 0:width] = dot(f2[a].reshape(256, 512), xe[a, :, 256 * e + lane:256 * e + lane + width]).astype(BF)

        loop(8, block)

        def group(n):
            q, rg = n // 4, n % 4
            rows = fmx[:, rows_at(n * 32, 32), 0:width].reshape(256, width)
            tiles = dot(to_col[...], rows).astype(BF).reshape(2, 4, 32, width)
            for h in range(2):
                fs[e, pl.ds(q * 32 + h * 16 + rg * 4, 4), :, lane:lane + width] = tiles[h]

        loop(8, group)
        lanes = slice(lane, lane + width)
        rsem = one["a1_rb" if e else "a1_ra"]
        pltpu.make_async_copy(fs.at[e, s, :, lanes], fm.at[e, s, :, lanes], rsem).start()

        def send(i):
            t = offset(s, i)
            remote(fs.at[e, t, :, lanes], fm.at[e, s, :, lanes], one["a1_s"], rsem, t, p).start()

        loop(64, send, 1)

    load_f.wait()
    drain(f2.at[:, 1 - side], one["f_r"])
    drain(sp.at[:, pl.ds(0, 2)], one["sa_r"])
    half = sp.at[:, pl.ds(base, 2)]
    remote(half, half, one["sb_s"], one["sb_r"], s, cross).start()
    first_mix(0, 0, 256)
    x_half(0).wait_send()
    x_half(1).start()
    x_half(0).wait_recv()
    first_mix(1, 0, 128)

    def mixed_columns(e):
        def piece(t):
            rows = fm[e, pl.ds(t * 16, 16)].astype(F32)
            for k in range(4):
                fmk[k, rows_at(t * 128, 128), 256 * e:256 * e + 256] = (
                    rows[:, 8 * k:8 * k + 8, :].reshape(128, 256).astype(BF)
                )

        loop(4, piece)

    def second_mix(e, k):
        def piece(t):
            mb[e, pl.ds(t * 16, 16), k] = pack(dot(sp[k, t], fmk[k, :, 256 * e:256 * e + 256]))

        loop(4, piece)

    drain(sp.at[:, pl.ds(0, 2)], one["sb_r"])
    drain(fs.at[0], one["a1_ra"])
    mixed_columns(0)
    for k in range(4):
        second_mix(0, k)
    pltpu.make_async_copy(mb.at[0, s], mr.at[0, s // 8, s % 8], one["a2_ra"]).start()

    def send_own(i):
        t = offset(s, i)
        remote(mb.at[0, t], mr.at[0, s // 8, s % 8], one["a2_sa"], one["a2_ra"], t, p).start()

    loop(64, send_own, 1)

    def turn_second(k):
        for t in range(4):
            for u in range(4):
                st[k, u, :, 128 * t:128 * t + 128] = sp[k, t, :, 128 * u:128 * u + 128].T

    loop(4, turn_second)

    x_half(1).wait_recv()
    first_mix(1, 128, 128)

    def tokens(rel, pick, shape):
        output, d_mixed, hid_part, out_part = token_tile(
            unpack(pick(mr)[...]), unpack(pick(xt)[...]), unpack(pick(ct)[...]), w1[...], w2[...], w1t[...], w2t[...]
        )
        pick(ob)[...] = pack(output).reshape(shape)
        pick(db)[...] = pack(d_mixed).reshape(shape)
        acc[0:16] += hid_part.reshape(16, 16, 768)
        acc[16:32] += out_part.reshape(16, 16, 768)

    drain(mb.at[0], one["a2_ra"])

    def own_tile(n):
        lo = (s + n) % 8
        tokens(0, lambda ref: ref.at[0, :, lo], (8, 4, 16, 128))

        def send(m):
            hi = (s // 8 + m) % 8
            t = hi * 8 + lo
            here = t == s

            @pl.when(here)
            def _():
                pltpu.make_async_copy(db.at[0, hi, lo], dr.at[0, s], one["a3_ra"]).start()

            @pl.when(jnp.logical_not(here))
            def _():
                remote(db.at[0, hi, lo], dr.at[0, s], one["a3_sa"], one["a3_ra"], t, p).start()

        loop(8, send)

    loop(4, own_tile)

    drain(fs.at[1], one["a1_rb"])
    mixed_columns(1)

    def mate_mix(k):
        second_mix(1, k)

        def send(i):
            t = offset(s, i)
            remote(mb.at[1, t, k], mr.at[1, s // 8, s % 8, k], four["a2_s"].at[k], four["a2_r"].at[k], t, mate).start()

        loop(64, send)

    for k in range(3):
        mate_mix(k)
    loop(8, own_tile, 4)

    def d_columns(e, k):
        def piece(t):
            dmk[k, rows_at(t * 128, 128), 256 * e:256 * e + 256] = unpack(dr[e, pl.ds(t * 16, 16), k]).astype(BF)

        loop(4, piece)

    def first_back(e, k):
        def piece(t):
            dfb[e, pl.ds(t * 16, 16), k] = pack(dot(st[k, t], dmk[k, :, 256 * e:256 * e + 256]))

        loop(4, piece)

    def own_back():
        drain(mb.at[0], one["a3_ra"])
        for k in range(4):
            d_columns(0, k)
            first_back(0, k)
        pltpu.make_async_copy(dfb.at[0, s], dfr.at[0, s], one["a4_ra"]).start()

        def send(i):
            t = offset(s, i)
            remote(dfb.at[0, t], dfr.at[0, s], one["a4_sa"], one["a4_ra"], t, p).start()

        loop(64, send, 1)

    def mate_tokens(k):
        drain(mb.at[1, :, k], four["a2_r"].at[k])

        def tile(n):
            lo = 4 * ((s // 4 + n) % 2)
            tokens(1, lambda ref: ref.at[1, :, pl.ds(lo, 4), k], (8, 4, 16, 128))

            def send(m):
                t = ((s // 8 + m) % 8) * 8 + lo + (s + m // 8) % 4
                remote(
                    db.at[1, t // 8, t % 8, k], dr.at[1, s, k], four["a3_s"].at[k], four["a3_r"].at[k], t, mate
                ).start()

            loop(32, send)

        loop(2, tile)

    def mate_back(k):
        drain(mb.at[1, :, k], four["a3_r"].at[k])
        d_columns(1, k)

        def piece(i):
            t = (2 - base + i) % 4
            gb[k, t] = dot(dmk[k, rows_at(t * 128, 128), :], fmk[k], ((1,), (1,))).astype(BF)

        loop(2, piece)
        remote(gb.at[k, pl.ds(2 - base, 2)], gr.at[k], four["g_s"].at[k], four["g_r"].at[k], s, cross).start()
        first_back(1, k)
        pltpu.make_async_copy(dfb.at[1, s, k], dfr.at[1, s, k], four["a4_r"].at[k]).start()

        def send(i):
            t = offset(s, i)
            remote(dfb.at[1, t, k], dfr.at[1, s, k], four["a4_s"].at[k], four["a4_r"].at[k], t, p).start()

        loop(64, send, 1)
        loop(4, piece, 2)

    def first_grad(k):
        drain(dfb.at[1, :, k], four["a4_r"].at[k])
        for e in range(2):
            for g in range(2):
                rows = unpack(dfr[e, 32 * g:32 * g + 32, k]).astype(BF)
                dfa[:, 32 * g:32 * g + 32, 256 * e:256 * e + 256] = (
                    dot(to_block[...], rows).astype(BF).reshape(8, 32, 256)
                )

        def block(a):
            fgb[k, :, a] = dot(dfa[a], xe[a], ((1,), (1,))).astype(BF).reshape(2, 32, 512)

        for part in (0, 4):
            loop(part + 4, block, part)
            away = fgb.at[k, 1 - side, pl.ds(part, 4)]
            remote(away, fgr.at[k, pl.ds(part, 4)], four["h_s"].at[k], four["h_r"].at[k], s, cross).start()

    def second_sum(k):
        drain(gr.at[k], four["g_r"].at[k])
        mine = gb[k, pl.ds(base, 2)].astype(F32)
        go[k] = ((mine + gr[k].astype(F32)) * BLOCK_SCALE).astype(BF)
        home = jnp.where(same, s, twin)
        remote(go.at[k, 1 - odd], sg_ref.at[4 * b + k], four["go_s0"].at[k], one["go_r"], home, mate).start()

        @pl.when(same)
        def _():
            pltpu.make_async_copy(go.at[k, odd], sg_ref.at[4 * b + k], one["go_r"]).start()

        @pl.when(unlike)
        def _():
            remote(go.at[k, odd], sg_ref.at[4 * b + k], four["go_s1"].at[k], one["go_r"], twin, p).start()

    w = s % 32

    def reduce_start():
        pltpu.make_async_copy(acc.at[w], rsb.at[w], one["rs_r"]).start()

        def send(i):
            t = (w + i) % 32
            remote(acc.at[t], rsb.at[w], one["rs_s"], one["rs_r"], z * 32 + t, p).start()

        loop(32, send, 1)

    def reduce_pair():
        drain(rsb, one["rs_r"])
        zl[0] = jnp.sum(rsb[...], axis=0)
        remote(zl.at[0], zl.at[1], one["zl_s"], one["zl_r"], flip, p).start()

    def reduce_planes():
        drain(zl.at[1], one["zl_r"])
        zb[p] = zl[0] + zl[1]
        for i in range(1, 4):
            remote(zb.at[p], zb.at[p], one["z_s"], one["z_r"], s, (p + i) % 4).start()

    def reduce_gather():
        drain(zb.at[pl.ds(0, 3)], one["z_r"])
        agb[w] = jnp.sum(zb[...], axis=0) * WEIGHT_SCALE

        def send(i):
            remote(agb.at[w], agb.at[w], one["ag_s"], one["ag_r"], z * 32 + (w + i) % 32, p).start()

        loop(32, send, 1)

    own_back()
    mate_tokens(0)
    mate_mix(3)
    mate_tokens(1)
    mate_back(0)
    mate_tokens(2)
    mate_back(1)
    drain(dfb.at[0], one["a4_ra"])
    first_grad(0)
    mate_tokens(3)
    reduce_start()
    mate_back(2)
    first_grad(1)
    second_sum(0)
    mate_back(3)
    reduce_pair()
    first_grad(2)
    second_sum(1)
    reduce_planes()
    first_grad(3)
    second_sum(2)
    reduce_gather()

    def to_rows(n):
        q, rg = n // 4, n % 4
        rel = (q // 2 + q % 2 + kind) % 2
        lo = (rg % 2) * 4
        hi = (q // 2) * 4 + rg // 2
        tiles = jnp.concatenate([ob[rel, hi, pl.ds(lo, 4)], ob[rel, hi + 2, pl.ds(lo, 4)]], axis=0)
        rows = dot(to_row[...], unpack(tiles).astype(BF)).astype(BF)
        raw[:, rows_at(n * 32, 32), :] = rows.reshape(8, 32, 256)

    loop(16, to_rows)
    for n in range(8):
        pltpu.make_async_copy(raw.at[n], out_ref.at[0, pl.ds(512 * n, 512)], one["t_out"]).start()

    second_sum(3)
    drain(agb.at[pl.ds(0, 31)], one["ag_r"])
    pltpu.make_async_copy(agb.at[pl.ds(0, 16)], hid_ref, one["t_hid"]).start()
    for n in range(6):
        wide[128 * n:128 * n + 128, :] = agb[16:32, :, 128 * n:128 * n + 128].reshape(256, 128).T
    pltpu.make_async_copy(wide, wide_ref, one["t_wide"]).start()

    for k in range(4):
        drain(fgr.at[k], four["h_r"].at[k])

    def first_sum(a):
        total = (fgb[:, side, a].astype(F32) + fgr[:, a].astype(F32)) * BLOCK_SCALE
        fgo[a] = dot(to_k[...], total.astype(BF).reshape(128, 512)).astype(BF)

    loop(8, first_sum)
    pltpu.make_async_copy(fgo, fg_ref, one["t_first"]).start()

    drain(f_ref, one["f_s"])
    drain(s_ref.at[0], one["sa_s0"])

    @pl.when(unlike)
    def _():
        drain(s_ref.at[0], one["sa_s1"])
        for k in range(4):
            drain(go.at[k, 0], four["go_s1"].at[k])

    drain(half, one["sb_s"])
    x_half(1).wait_send()
    drain(fs.at[:, pl.ds(0, 63)], one["a1_s"])
    for name in ("a2_sa", "a3_sa", "a4_sa"):
        drain(mb.at[0, pl.ds(0, 63)], one[name])
    for k in range(4):
        drain(mb.at[1, :, k], four["a2_s"].at[k])
        drain(mb.at[1, :, k], four["a3_s"].at[k])
        drain(mb.at[1, pl.ds(0, 63), k], four["a4_s"].at[k])
        drain(gr.at[k], four["g_s"].at[k])
        drain(fgr.at[k], four["h_s"].at[k])
        drain(go.at[k, 0], four["go_s0"].at[k])
    drain(rsb.at[pl.ds(0, 31)], one["rs_s"])
    drain(zl.at[0], one["zl_s"])
    drain(zb.at[pl.ds(0, 3)], one["z_s"])
    drain(agb.at[pl.ds(0, 31)], one["ag_s"])
    drain(sg_ref, one["go_r"])
    drain(raw, one["t_out"])
    drain(fgo, one["t_first"])
    drain(agb.at[pl.ds(0, 16)], one["t_hid"])
    drain(wide, one["t_wide"])


def permutation(*shape_and_order):
    shape, order = shape_and_order
    places = np.arange(math.prod(shape)).reshape(shape).transpose(order).reshape(-1)
    return np.eye(places.size, dtype=np.float32)[places]


def local(tokens, cotangent, first_factor, second_factor, hidden_weight, output_weight):
    to_col = permutation((8, 4, 2, 4), (2, 1, 3, 0))
    to_block = permutation((32, 8), (1, 0))
    to_k = permutation((4, 2, 16), (2, 1, 0))
    tiles = (2, 8, 8, 4, 16, 128)
    pieces = (2, 64, 4, 16, 128)
    scratch = [
        ((8, 512, 512), BF), ((8, 512, 256), BF), ((8, 2, 128, 512), BF), ((8, 256, 256), BF),
        ((2, 64, 32, 256), BF), ((2, 64, 32, 256), BF), ((4, 512, 512), BF),
        ((4, 4, 128, 512), BF), ((4, 4, 128, 512), BF),
        (tiles, BF), (tiles, BF), (tiles, BF), (pieces, BF), (tiles, BF), (tiles, BF), (pieces, BF),
        ((4, 512, 512), BF), (pieces, BF), (pieces, BF), ((8, 64, 512), BF),
        ((4, 4, 128, 512), BF), ((4, 2, 128, 512), BF), ((4, 2, 128, 512), BF),
        ((4, 2, 8, 32, 512), BF), ((4, 8, 32, 512), BF), ((8, 128, 512), BF),
        ((32, 16, 768), F32), ((32, 16, 768), F32), ((2, 16, 768), F32), ((4, 16, 768), F32), ((32, 16, 768), F32),
        ((768, 256), F32), ((768, 256), BF), ((256, 768), BF),
    ]
    out, fg, sg, hid, wide = pl.pallas_call(
        kernel,
        out_shape=(
            jax.ShapeDtypeStruct((1, 4096, 256), BF),
            jax.ShapeDtypeStruct((8, 128, 512), BF),
            jax.ShapeDtypeStruct((8, 128, 512), BF),
            jax.ShapeDtypeStruct((16, 16, 768), F32),
            jax.ShapeDtypeStruct((768, 256), F32),
        ),
        in_specs=[ANY] * 4 + [VM] * 6,
        out_specs=(ANY,) * 5,
        scratch_shapes=[pltpu.VMEM(*shape) for shape in scratch]
        + [DMA((len(SINGLES),)), DMA((len(FOURS), 4))],
        compiler_params=pltpu.CompilerParams(
            collective_id=1, has_side_effects=True, vmem_limit_bytes=62 << 20
        ),
    )(
        tokens.reshape(8, 512, 256), cotangent.reshape(8, 512, 256), first_factor,
        second_factor.reshape(2, 4, 128, 512), hidden_weight, output_weight,
        jnp.asarray(to_col, BF), jnp.asarray(to_col.T, BF), jnp.asarray(to_block, BF), jnp.asarray(to_k, BF),
    )
    return out, fg, sg, hid.reshape(256, 768), wide


def solution(mesh):
    in_specs = (
        P("dp", "seq", None),
        P("dp", "seq", None),
        P("seq", "dp", None),
        P("seq", "dp", None),
        P(),
        P(),
    )
    out_specs = (P("dp", "seq", None), P("seq", "dp", None), P("seq", "dp", None), P(), P())
    return jax.shard_map(local, mesh=mesh, in_specs=in_specs, out_specs=out_specs, check_vma=False)
```
